32 devices in a mesh: src: 4 (over y, core), vocab: 8 (over z, x).
Axes of the slice: x: 2, y: 2, z: 4, core: 2. Of those that a mesh axis runs over, the one named last changes fastest.
Arguments:
- queries: bfloat16 [2048, 2048], P('vocab', 'src'), may hold values from -35 to 35
- enc_keys: bfloat16 [8, 256, 2048], P('vocab', None, 'src'), may hold values from -4 to 4
- enc_values: bfloat16 [8, 256, 2048], P('vocab', None, 'src'), may hold values from -48 to 48
- source_lengths: int32 [8], P('vocab'), may hold values from 1 to 256, 1024 in all
- out_proj: bfloat16 [2048, 2048], P('src'), may hold values from -0.125 to 0.125
- dec_state: bfloat16 [2048, 2048], P('vocab', 'src'), may hold values from -24 to 24
- norm_gain: float32 [2048], P('src'), may hold values from 0.25 to 1.75
- norm_bias: float32 [2048], P('src'), may hold values from -3 to 3
- head_weight: bfloat16 [2048, 64512], P('src', 'vocab'), may hold values from -2 to 2
- shortlist: int32 [2048, 8], P('vocab'), may hold values from 0 to 503, all different within a row; in each aligned block of 256 rows (0 to 255, 256 to 511, ...) at most 8 rows name the same one
- target_slot: int32 [2048], P('vocab'), may hold values from 0 to 7
- target_offset: int32 [2048], P('vocab'), may hold values from 0 to 127
Outputs:
- row_loss: float32 [2048], P('vocab')
- grad_state: float32 [2048, 2048], P('vocab', 'src')
The draws below stay inside these ranges and needn't reach their ends.
Inputs may be any that keep to these rules, and one draw needn't show every extreme that they name: `shortlist`: each row lists 8 different blocks; the rows of one sentence list one block at most 8 times.
All inputs are finite; a program needn't handle non-finite values. No bound on the sum of `source_lengths` on one device may be relied on, other than what follows from the above.
Results may differ from the reference program's by a relative error of at most 0.0055.
Values may be sent and summed in bfloat16 or wider, within the bound.
A program may use at most 64 MiB of HBM per device.

```python
import math
import jax
import jax.numpy as jnp
import numpy as np
from jax import lax

D = 2048
H = 16
HD = 128
BLK = 128
K_LIST = 8
ROWS_DEV = 256
SRC_LEN = 256
SEQS = 8
TGT_ROWS = 2048
VOCAB_BLOCKS = 504
VOCAB = 64512
MOST = 8


def leading_keys(key):
    root_key = jax.random.fold_in(key, 17)
    first_key, rest_key = jax.random.split(root_key)
    front_rows = jnp.clip(jax.random.normal(first_key, (SEQS, 2, D), jnp.float32), -4.0, 4.0)
    return (front_rows, rest_key)


def draw_enc_keys(key, part):
    front_rows, rest_key = leading_keys(key)
    others = jnp.clip(jax.random.normal(rest_key, (SEQS, SRC_LEN - 2, D), jnp.float32), -4.0, 4.0)
    return jnp.concatenate([front_rows, others], axis=1).astype(jnp.bfloat16)


def draw_queries(key, part):
    root_key = jax.random.fold_in(key, 23)
    first_key = jax.random.fold_in(root_key, 0)
    values_field = jnp.clip(jax.random.normal(first_key, (TGT_ROWS, D), jnp.float32), -4.0, 4.0)
    return values_field.astype(jnp.bfloat16)


def draw_dec_state(key, part):
    root_key = jax.random.fold_in(key, 31)
    first_key, second_key, third_key = jax.random.split(root_key, 3)
    row_scales = jnp.exp(jax.random.uniform(first_key, (TGT_ROWS, 1), jnp.float32, -1.3863, 0.9163))
    placing = jnp.arange(D, dtype=jnp.float32) / D
    col_rough = jnp.exp(jax.random.uniform(second_key, (D,), jnp.float32, -0.5108, 0.47))
    col_scales = 3.0 ** (placing - 0.5) * col_rough
    noises = jnp.clip(jax.random.normal(third_key, (TGT_ROWS, D), jnp.float32), -3.0, 3.0)
    values_field = noises * row_scales * col_scales
    return jnp.clip(values_field, -24.0, 24.0).astype(jnp.bfloat16)


def draw_head_weight(key, part):
    root_key = jax.random.fold_in(key, 47)
    scaling = 3.0 / D ** 0.5
    weights = jnp.clip(jax.random.normal(root_key, (D, VOCAB), jnp.float32), -4.0, 4.0) * scaling
    return weights.astype(jnp.bfloat16)


def with_ends(values, own_key, smallest, high):
    place = [jax.random.randint(jax.random.fold_in(own_key, axis), (), 0, length) for axis, length in enumerate(values.shape)]
    main_axis = values.shape.index(max(values.shape))
    neighbour = place[:main_axis] + [(place[main_axis] + 1) % values.shape[main_axis]] + place[main_axis + 1:]
    return values.at[tuple(place)].set(smallest).at[tuple(neighbour)].set(high)


def block_scale(stream_key, extent, cuts, least, high):
    level, own = 1.0, jax.random.fold_in(stream_key, 6)
    for position, blocks in cuts:
        steps = jnp.exp(jax.random.uniform(jax.random.fold_in(own, position), (blocks,), jnp.float32, least / len(cuts), high / len(cuts)))
        level = level * jnp.repeat(steps, extent[position] // blocks).reshape([-1 if axis == position else 1 for axis in range(len(extent))])
    return level


def profile(count, total, reach, slope):
    portions = [(1 << 20) // math.isqrt(grade ** slope) + 1 for grade in range(2, count + 1)]
    rest, given = total - reach - (count - 1), [1] * (count - 1)
    while rest > 0:
        free = [i for i in range(count - 1) if given[i] < reach]
        mass, left = sum([portions[i] for i in free]), rest
        for i in free:
            addition = min(reach - given[i], max(1, left * portions[i] // mass), rest)
            given[i] = given[i] + addition
            rest = rest - addition
    return np.array([reach] + given)


def uneven(own_key, amount, total, bound, lean):
    if amount == 2:
        one = jax.random.randint(own_key, (), max(1, total - bound), min(bound, total - 1) + 1)
        return jnp.stack([one, total - one])
    lengths = jnp.asarray(profile(amount, total, bound, lean), jnp.int32)
    twos = (amount - 1) // 2
    donor, receiver = lengths[1:1 + 2 * twos:2], lengths[2:2 + 2 * twos:2]
    room = jnp.minimum(donor - 1, bound - receiver)
    moved = jax.random.randint(jax.random.fold_in(own_key, 1), (twos,), 0, 1 << 20) % (room + 1)
    lengths = lengths.at[1:1 + 2 * twos:2].set(donor - moved).at[2:2 + 2 * twos:2].set(receiver + moved)
    return lengths[jax.random.permutation(jax.random.fold_in(own_key, 2), amount)]


def shared_out(rng, own, number, rows, count, top, most, slope):
    order = jax.random.permutation(rng, count)
    crowded, usual = load_shares(count, rows * top, most, slope, True), load_shares(count, rows * top, most, slope, False)
    places = jnp.arange(count)

    def named(sizes, offset_by):
        used = int((sizes > 0).sum())
        fixed = max(1, used // 4)
        shifted = fixed + (places - fixed + offset_by * (used - fixed)) % max(1, count - fixed)
        return jnp.zeros((count,), jnp.int32).at[order[jnp.where(places < fixed, places, shifted)]].set(jnp.asarray(sizes, jnp.int32))

    sizes = jnp.where(number % 4 == 0, named(crowded, number // 4), named(usual, number - number // 4 - 1))
    mixed = jax.random.permutation(jax.random.fold_in(own, 3), count)
    source_of, taker = mixed[0:count // 2 * 2:2], mixed[1:count // 2 * 2:2]
    margin = jnp.minimum(sizes[source_of] - 1, most - sizes[taker]) // 2
    margin = jnp.where((source_of == order[0]) | (taker == order[0]) | (sizes[taker] == 0), 0, jnp.maximum(margin, 0))
    shifted = jax.random.randint(jax.random.fold_in(own, 4), (count // 2,), 0, 1 << 20) % (margin + 1)
    sizes = sizes.at[source_of].add(-shifted).at[taker].add(shifted)
    members = jnp.searchsorted(jnp.cumsum(sizes), jnp.arange(rows * top), side="right").astype(jnp.int32)
    table = members.reshape(top, rows).T
    table = table[jax.random.permutation(jax.random.fold_in(own, 1), rows)]
    offset_by = jax.random.randint(jax.random.fold_in(own, 2), (rows, 1), 0, top)
    return jnp.take_along_axis(table, (jnp.arange(top)[None, :] + offset_by) % top, axis=1)


def load_shares(count, total, reach, slope, full):
    portions = [(1 << 20) // math.isqrt(rank ** slope) + 1 for rank in range(1, count + 1)]
    largest = reach if full else min(reach, max(-(-total // count), total * portions[0] // sum(portions)))
    least = 1 if total - largest >= count - 1 else 0
    holding, spare = [largest] + [least] * (count - 1), total - largest - least * (count - 1)
    while spare > 0:
        candidates = [i for i in range(1, count) if holding[i] < largest] or [i for i in range(1, count) if holding[i] < reach]
        mass, remaining = sum([portions[i] for i in candidates]), spare
        for i in candidates:
            addition = min(reach - holding[i], max(1, remaining * portions[i] // mass), spare)
            holding[i] = holding[i] + addition
            spare = spare - addition
    return np.array(holding)


def noise(own_key, shape, scale, reach, pieces=(), kind=jnp.bfloat16):
    array = jax.random.normal(own_key, shape, jnp.float32) * scale
    if len(pieces) > 0:
        array = block_scale(own_key, shape, pieces, -0.22, 0.18) * array
    return jnp.clip(array, min=-reach, max=reach).astype(kind)


def setup_inputs(seed: int = 0) -> dict:
    arg_keys = jax.random.split(jax.random.key(seed), 13)
    queries = draw_queries(jax.random.fold_in(arg_keys[12], 71), 0)
    enc_keys = draw_enc_keys(jax.random.fold_in(arg_keys[12], 71), 0)
    enc_values = noise(arg_keys[2], (SEQS, SRC_LEN, D), 8.0, 48.0, ((0, 8), (2, 4)))
    source_lengths = uneven(arg_keys[3], SEQS, SEQS * SRC_LEN // 2, SRC_LEN, 2).astype(jnp.int32)
    out_proj = noise(arg_keys[4], (D, D), D ** -0.5, 0.125, ((0, 4),))
    dec_state = draw_dec_state(jax.random.fold_in(arg_keys[12], 71), 0)
    norm_gain = jnp.clip(1.0 + 0.15 * jax.random.normal(arg_keys[6], (D,), jnp.float32), 0.25, 1.75)
    norm_bias = noise(arg_keys[7], (D,), 0.5, 3.0, ((0, 4),), jnp.float32)
    head_weight = draw_head_weight(jax.random.fold_in(arg_keys[12], 71), 0)
    shortlist_keys = jax.random.split(jax.random.fold_in(arg_keys[9], 1), TGT_ROWS // ROWS_DEV)
    shortlist_turns = jax.random.permutation(jax.random.fold_in(arg_keys[9], 3), TGT_ROWS // ROWS_DEV)
    shortlist = jax.vmap(lambda own, number: shared_out(jax.random.fold_in(arg_keys[9], 2), own, number, ROWS_DEV, VOCAB_BLOCKS, K_LIST, MOST, 2))(shortlist_keys, shortlist_turns).reshape((TGT_ROWS, K_LIST))
    target_slot = with_ends(jax.random.randint(arg_keys[10], (TGT_ROWS,), 0, K_LIST), jax.random.fold_in(arg_keys[10], 1), 0, K_LIST - 1).astype(jnp.int32)
    target_offset = with_ends(jax.random.randint(arg_keys[11], (TGT_ROWS,), 0, BLK), jax.random.fold_in(arg_keys[11], 1), 0, BLK - 1).astype(jnp.int32)
    return {"queries": queries, "enc_keys": enc_keys, "enc_values": enc_values, "source_lengths": source_lengths, "out_proj": out_proj, "dec_state": dec_state, "norm_gain": norm_gain, "norm_bias": norm_bias, "head_weight": head_weight, "shortlist": shortlist, "target_slot": target_slot, "target_offset": target_offset}


MASKED = -1e+30
EPSILON = 1e-05

def attend_sequence(inputs):
    query_rows, key_rows, value_rows, length = inputs
    scaling = 1.0 / math.sqrt(HD)
    queries_f = query_rows.reshape(ROWS_DEV, H, HD).astype(jnp.float32)
    keys_f = key_rows.reshape(SRC_LEN, H, HD).astype(jnp.float32)
    values_f = value_rows.reshape(SRC_LEN, H, HD).astype(jnp.float32)
    scores = jnp.einsum('rhe,phe->hrp', queries_f, keys_f) * scaling
    usable = (jnp.arange(SRC_LEN, dtype=jnp.int32) < length)[None, None, :]
    scores = jnp.where(usable, scores, MASKED)
    row_top = lax.optimization_barrier(jnp.max(scores, axis=-1, keepdims=True))
    raw_weights = jnp.where(usable, jnp.exp(scores - row_top), 0.0)
    totals = lax.optimization_barrier(jnp.sum(raw_weights, axis=-1))
    rounded = lax.optimization_barrier(raw_weights.astype(jnp.bfloat16)).astype(jnp.float32)
    mixture = jnp.einsum('hrp,phe->rhe', rounded, values_f)
    return (mixture / totals.T[:, :, None]).astype(jnp.bfloat16).reshape(ROWS_DEV, D)

def reference(queries, enc_keys, enc_values, source_lengths, out_proj, dec_state, norm_gain, norm_bias, head_weight, shortlist, target_slot, target_offset):
    attended = lax.map(attend_sequence, (queries.reshape(SEQS, ROWS_DEV, D), enc_keys, enc_values, source_lengths))
    attended = attended.reshape(TGT_ROWS, D)
    residual = dec_state.astype(jnp.float32) + jnp.dot(attended, out_proj, preferred_element_type=jnp.float32)
    row_mean = lax.optimization_barrier(jnp.mean(residual, axis=1, keepdims=True))
    variance = lax.optimization_barrier(jnp.mean((residual - row_mean) ** 2, axis=1, keepdims=True))
    inv_std = lax.rsqrt(variance + EPSILON)
    centered = (residual - row_mean) * inv_std
    normed = lax.optimization_barrier((centered * norm_gain + norm_bias).astype(jnp.bfloat16))
    columns = head_weight.reshape(D, VOCAB_BLOCKS, BLK)

    def score_rows(inputs):
        normed_rows, listed, slot_rows, offset_rows = inputs
        picked_cols = jnp.take(columns, listed, axis=1).astype(jnp.float32)
        logits = jnp.einsum('rd,drkt->rkt', normed_rows.astype(jnp.float32), picked_cols)
        row_best = lax.optimization_barrier(jnp.max(logits, axis=(1, 2)))
        log_total = row_best + jnp.log(lax.optimization_barrier(jnp.sum(jnp.exp(logits - row_best[:, None, None]), axis=(1, 2))))
        list_hit = jnp.arange(K_LIST, dtype=jnp.int32)[None, :, None] == slot_rows[:, None, None]
        place_hit = jnp.arange(BLK, dtype=jnp.int32)[None, None, :] == offset_rows[:, None, None]
        target_hit = jnp.logical_and(list_hit, place_hit)
        chosen = lax.optimization_barrier(jnp.sum(jnp.where(target_hit, logits, 0.0), axis=(1, 2)))
        deltas = jnp.exp(logits - log_total[:, None, None]) - target_hit.astype(jnp.float32)
        deltas = lax.optimization_barrier(deltas.astype(jnp.bfloat16)).astype(jnp.float32)
        grads = jnp.einsum('rkt,drkt->rd', deltas, picked_cols)
        return (log_total - chosen, grads)
    group_count = TGT_ROWS // 8
    losses, grad_normed = lax.map(score_rows, (normed.reshape(group_count, 8, D), shortlist.reshape(group_count, 8, K_LIST), target_slot.reshape(group_count, 8), target_offset.reshape(group_count, 8)))
    row_loss = losses.reshape(TGT_ROWS)
    grad_normed = grad_normed.reshape(TGT_ROWS, D)
    gained = grad_normed * norm_gain
    mean_g = lax.optimization_barrier(jnp.mean(gained, axis=1, keepdims=True))
    mean_gx = lax.optimization_barrier(jnp.mean(gained * centered, axis=1, keepdims=True))
    grad_state = inv_std * (gained - mean_g - centered * mean_gx)
    return (row_loss, grad_state)
```

```python
import math

import jax
import jax.numpy as jnp
from jax import lax
from jax.sharding import PartitionSpec as P

HD = 128
BLK = 128


MASKED = -1e30
EPSILON = 1e-05


def shards(
    queries,
    enc_keys,
    enc_values,
    source_lengths,
    out_proj,
    dec_state,
    norm_gain,
    norm_bias,
    head_weight,
    shortlist,
    target_slot,
    target_offset,
):
    voc_count = lax.axis_size("vocab")
    row_count = queries.shape[0]
    mem_count = enc_keys.shape[1]
    model_width = out_proj.shape[1]
    width_dev = dec_state.shape[1]
    heads_dev = enc_keys.shape[2] // HD
    facts = lax.all_gather(
        jnp.concatenate([shortlist.T, target_slot[None], target_offset[None]], axis=0),
        "vocab",
        axis=0,
    )
    q_heads = queries.reshape(row_count, heads_dev, HD)
    key_heads = enc_keys[0].reshape(mem_count, heads_dev, HD)
    value_heads = enc_values[0].reshape(mem_count, heads_dev, HD)
    scores = jnp.einsum("rhe,phe->hrp", q_heads, key_heads, preferred_element_type=jnp.float32) * (
        1.0 / math.sqrt(HD)
    )
    positions = lax.iota(jnp.int32, mem_count)
    usable = (positions < source_lengths[0])[None, None, :]
    scores = jnp.where(usable, scores, MASKED)
    row_top = jnp.max(scores, axis=-1)
    raw_weights = jnp.where(usable, jnp.exp(scores - row_top[..., None]), 0.0)
    totals = jnp.sum(raw_weights, axis=-1)
    mixture = jnp.einsum(
        "hrp,phe->rhe",
        raw_weights.astype(jnp.bfloat16),
        value_heads,
        preferred_element_type=jnp.float32,
    )
    own_mix = mixture / totals.T[..., None]
    attn_own = own_mix.astype(jnp.bfloat16).reshape(row_count, heads_dev * HD)
    projected = lax.psum_scatter(
        lax.dot_general(
            out_proj, attn_own, (((0,), (1,)), ((), ())), preferred_element_type=jnp.float32
        ),
        "src",
        scatter_dimension=0,
        tiled=True,
    )
    residual = dec_state.astype(jnp.float32) + projected.T
    sum_rows, square_rows = lax.psum(
        (jnp.sum(residual, axis=1), jnp.sum(residual * residual, axis=1)), "src"
    )
    row_mean = sum_rows / model_width
    variance = square_rows / model_width - row_mean * row_mean
    inv_std = lax.rsqrt(variance + EPSILON)
    centered = (residual - row_mean[:, None]) * inv_std[:, None]
    normed = (centered * norm_gain + norm_bias).astype(jnp.bfloat16)
    list_count = shortlist.shape[1]
    blocks_dev = head_weight.shape[1] // BLK
    vocab_blocks = blocks_dev * voc_count
    bucket_most = max(2, 2 * row_count * list_count // vocab_blocks)
    voc_own = lax.axis_index("vocab")
    local_ids = facts[:, :list_count] - voc_own * blocks_dev
    block_iota = lax.broadcasted_iota(jnp.int32, (1, blocks_dev, 1), 1)
    lists = jnp.zeros((voc_count, blocks_dev, row_count), jnp.bool_)
    codes = jnp.full((voc_count, blocks_dev, row_count), -1, jnp.int32)
    for k in range(list_count):
        named = local_ids[:, k][:, None, :] == block_iota
        lists = lists | named
        aimed = named & (facts[:, list_count] == k)[:, None, :]
        codes = jnp.where(aimed, facts[:, list_count + 1][:, None, :], codes)
    earlier = (
        lax.broadcasted_iota(jnp.int32, (row_count, row_count), 0)
        < lax.broadcasted_iota(jnp.int32, (row_count, row_count), 1)
    ).astype(jnp.bfloat16)
    ranks = jnp.einsum(
        "slr,rq->slq", lists.astype(jnp.bfloat16), earlier, preferred_element_type=jnp.float32
    ).astype(jnp.int32)
    rank_iota = lax.broadcasted_iota(jnp.int32, (1, 1, bucket_most, 1), 2)
    holds = lists[:, :, None, :] & (ranks[:, :, None, :] == rank_iota)
    places = holds.astype(jnp.bfloat16)
    slot_codes = jnp.max(jnp.where(holds, codes[:, :, None, :], -1), axis=3)
    normed_all = lax.all_gather(normed, "vocab", axis=0)
    received = jnp.einsum(
        "slmr,srd->slmd", places, normed_all, preferred_element_type=jnp.float32
    ).astype(jnp.bfloat16)
    weight_view = head_weight.reshape(width_dev, blocks_dev, BLK)
    partial_logits = jnp.einsum(
        "slmd,dlt->slmt", received, weight_view, preferred_element_type=jnp.float32
    )
    full_logits = lax.psum(partial_logits, "src")
    slot_top = jnp.max(full_logits, axis=3)
    row_high = jnp.max(jnp.where(holds, slot_top[..., None], MASKED), axis=(1, 2))
    slot_high = jnp.sum(jnp.where(holds, row_high[:, None, None, :], 0.0), axis=3)
    slot_spread = jnp.sum(jnp.exp(full_logits - slot_high[..., None]), axis=3)
    offsets = lax.broadcasted_iota(jnp.int32, full_logits.shape, 3)
    target_hit = offsets == slot_codes[..., None]
    slot_pick = jnp.sum(jnp.where(target_hit, full_logits, 0.0), axis=3)
    row_spread = jnp.sum(jnp.where(holds, slot_spread[..., None], 0.0), axis=(1, 2))
    row_pick = jnp.sum(jnp.where(holds, slot_pick[..., None], 0.0), axis=(1, 2))
    stats = lax.all_gather(jnp.stack([row_high, row_spread, row_pick]), "vocab", axis=0)
    best = jnp.max(stats[:, 0], axis=0)
    log_total = best + jnp.log(jnp.sum(jnp.exp(stats[:, 0] - best) * stats[:, 1], axis=0))
    row_loss = lax.dynamic_index_in_dim(
        log_total - jnp.sum(stats[:, 2], axis=0), voc_own, axis=0, keepdims=False
    )
    slot_total = jnp.sum(jnp.where(holds, log_total[:, None, None, :], 0.0), axis=3)
    deltas = (
        jnp.exp(full_logits - slot_total[..., None]) - target_hit.astype(jnp.float32)
    ).astype(jnp.bfloat16)
    grad_slots = jnp.einsum(
        "slmt,dlt->slmd", deltas, weight_view, preferred_element_type=jnp.float32
    ).astype(jnp.bfloat16)
    grad_rows = jnp.einsum(
        "slmr,slmd->srd", places, grad_slots, preferred_element_type=jnp.float32
    ).astype(jnp.bfloat16)
    returned = lax.all_to_all(grad_rows, "vocab", split_axis=0, concat_axis=0, tiled=True)
    grad_normed = jnp.sum(returned.astype(jnp.float32), axis=0)
    gained = grad_normed * norm_gain
    sum_g, sum_gx = lax.psum((jnp.sum(gained, axis=1), jnp.sum(gained * centered, axis=1)), "src")
    grad_state = inv_std[:, None] * (
        gained - (sum_g / model_width)[:, None] - centered * (sum_gx / model_width)[:, None]
    )
    return (row_loss, grad_state)


def solution(mesh):
    placed = (
        P("vocab", "src"),
        P("vocab", None, "src"),
        P("vocab", None, "src"),
        P("vocab"),
        P("src", None),
        P("vocab", "src"),
        P("src"),
        P("src"),
        P("src", "vocab"),
        P("vocab", None),
        P("vocab"),
        P("vocab"),
    )
    return jax.shard_map(
        shards,
        mesh=mesh,
        in_specs=placed,
        out_specs=(P("vocab"), P("vocab", "src")),
        check_vma=False,
    )
```

```python
import functools
import math

import jax
import jax.numpy as jnp
from jax import lax
from jax.experimental import pallas as pl
from jax.experimental.pallas import tpu as pltpu
from jax.sharding import PartitionSpec as P

HD = 128
BLK = 128


MASKED = -1e30
EPSILON = 1e-05


VMEM_BYTES = 40 * 1024 * 1024
MESH_ID = pl.DeviceIdType.MESH


def greet(axis, partners):
    barrier = pltpu.get_barrier_semaphore()
    for partner in partners:
        pl.semaphore_signal(barrier, inc=1, device_id={axis: partner}, device_id_type=MESH_ID)
    pl.semaphore_wait(barrier, len(partners))


def remote(axis, src, dst, send_sem, recv_sem, partner):
    return pltpu.make_async_remote_copy(
        src_ref=src,
        dst_ref=dst,
        send_sem=send_sem,
        recv_sem=recv_sem,
        device_id={axis: partner},
        device_id_type=MESH_ID,
    )


def gather_body(axis, count, own_ref, all_ref, send_sems, recv_sems):
    me = lax.axis_index(axis)
    partners = [lax.rem(me + step, count) for step in range(1, count)]
    greet(axis, partners)
    copies = []
    for i, partner in enumerate(partners):
        copy = remote(
            axis, own_ref, all_ref.at[me], send_sems.at[i], recv_sems.at[i], partner
        )
        copy.start()
        copies.append(copy)
    all_ref[me] = own_ref[...]
    for copy in copies:
        copy.wait()


def gather_small(own, axis, collective_id):
    count = lax.axis_size(axis)
    return pl.pallas_call(
        functools.partial(gather_body, axis, count),
        out_shape=jax.ShapeDtypeStruct((count,) + own.shape, own.dtype),
        in_specs=[pl.BlockSpec(memory_space=pltpu.VMEM)],
        out_specs=pl.BlockSpec(memory_space=pltpu.VMEM),
        scratch_shapes=[
            pltpu.SemaphoreType.DMA((count - 1,)),
            pltpu.SemaphoreType.DMA((count - 1,)),
        ],
        compiler_params=pltpu.CompilerParams(
            collective_id=collective_id, has_side_effects=True, vmem_limit_bytes=VMEM_BYTES
        ),
    )(own)


def src_places(axis, rings):
    me = lax.axis_index(axis)
    core = lax.rem(me, 2)
    ring = me // 2
    mate = me + 1 - 2 * core
    others = [lax.rem(ring + step, rings) for step in range(1, rings)]
    greet(axis, [mate] + [other * 2 + core for other in others])
    return core, ring, mate, others


def scatter_body(axis, rings, x_ref, o_ref, first, summed, second, sems):
    core, ring, mate, others = src_places(axis, rings)
    targets = others + [ring]
    pairs = []
    for i, target in enumerate(targets):
        copy = remote(
            axis, x_ref.at[target * 2 + 1 - core], first.at[i], sems.at[0, i], sems.at[1, i], mate
        )
        copy.start()
        pairs.append(copy)
    crossings = []
    for i, target in enumerate(others):
        pairs[i].wait_recv()
        summed[i] = x_ref[target * 2 + core] + first[i]
        copy = remote(
            axis, summed.at[i], second.at[i], sems.at[2, i], sems.at[3, i], target * 2 + core
        )
        copy.start()
        crossings.append(copy)
    pairs[-1].wait_recv()
    o_ref[...] = x_ref[ring * 2 + core] + first[rings - 1]
    for i, copy in enumerate(crossings):
        copy.wait_recv()
        o_ref[...] += second[i]
    for copy in pairs + crossings:
        copy.wait_send()


def scatter_sum(chunks, axis, collective_id):
    count = chunks.shape[0]
    rings = count // 2
    piece = chunks.shape[1:]
    crossing = max(rings - 1, 1)
    return pl.pallas_call(
        functools.partial(scatter_body, axis, rings),
        out_shape=jax.ShapeDtypeStruct(piece, chunks.dtype),
        in_specs=[pl.BlockSpec(memory_space=pltpu.VMEM)],
        out_specs=pl.BlockSpec(memory_space=pltpu.VMEM),
        scratch_shapes=[
            pltpu.VMEM((rings,) + piece, chunks.dtype),
            pltpu.VMEM((crossing,) + piece, chunks.dtype),
            pltpu.VMEM((crossing,) + piece, chunks.dtype),
            pltpu.SemaphoreType.DMA((4, rings)),
        ],
        compiler_params=pltpu.CompilerParams(
            collective_id=collective_id, has_side_effects=True, vmem_limit_bytes=VMEM_BYTES
        ),
    )(chunks)


def shards(
    queries,
    enc_keys,
    enc_values,
    source_lengths,
    out_proj,
    dec_state,
    norm_gain,
    norm_bias,
    head_weight,
    shortlist,
    target_slot,
    target_offset,
):
    voc_count = lax.axis_size("vocab")
    row_count = queries.shape[0]
    mem_count = enc_keys.shape[1]
    model_width = out_proj.shape[1]
    width_dev = dec_state.shape[1]
    heads_dev = enc_keys.shape[2] // HD
    facts = gather_small(
        jnp.concatenate([shortlist.T, target_slot[None], target_offset[None]], axis=0), "vocab", 1
    )
    q_heads = queries.reshape(row_count, heads_dev, HD)
    key_heads = enc_keys[0].reshape(mem_count, heads_dev, HD)
    value_heads = enc_values[0].reshape(mem_count, heads_dev, HD)
    scores = jnp.einsum("rhe,phe->hrp", q_heads, key_heads, preferred_element_type=jnp.float32) * (
        1.0 / math.sqrt(HD)
    )
    positions = lax.iota(jnp.int32, mem_count)
    usable = (positions < source_lengths[0])[None, None, :]
    scores = jnp.where(usable, scores, MASKED)
    row_top = jnp.max(scores, axis=-1)
    raw_weights = jnp.where(usable, jnp.exp(scores - row_top[..., None]), 0.0)
    totals = jnp.sum(raw_weights, axis=-1)
    mixture = jnp.einsum(
        "hrp,phe->rhe",
        raw_weights.astype(jnp.bfloat16),
        value_heads,
        preferred_element_type=jnp.float32,
    )
    own_mix = mixture / totals.T[..., None]
    attn_own = own_mix.astype(jnp.bfloat16).reshape(row_count, heads_dev * HD)
    projected = scatter_sum(
        lax.dot_general(
            out_proj, attn_own, (((0,), (1,)), ((), ())), preferred_element_type=jnp.float32
        ).reshape(-1, width_dev, row_count),
        "src",
        2,
    )
    residual = dec_state.astype(jnp.float32) + projected.T
    sum_rows, square_rows = lax.psum(
        (jnp.sum(residual, axis=1), jnp.sum(residual * residual, axis=1)), "src"
    )
    row_mean = sum_rows / model_width
    variance = square_rows / model_width - row_mean * row_mean
    inv_std = lax.rsqrt(variance + EPSILON)
    centered = (residual - row_mean[:, None]) * inv_std[:, None]
    normed = (centered * norm_gain + norm_bias).astype(jnp.bfloat16)
    list_count = shortlist.shape[1]
    blocks_dev = head_weight.shape[1] // BLK
    vocab_blocks = blocks_dev * voc_count
    bucket_most = max(2, 2 * row_count * list_count // vocab_blocks)
    voc_own = lax.axis_index("vocab")
    local_ids = facts[:, :list_count] - voc_own * blocks_dev
    block_iota = lax.broadcasted_iota(jnp.int32, (1, blocks_dev, 1), 1)
    lists = jnp.zeros((voc_count, blocks_dev, row_count), jnp.bool_)
    codes = jnp.full((voc_count, blocks_dev, row_count), -1, jnp.int32)
    for k in range(list_count):
        named = local_ids[:, k][:, None, :] == block_iota
        lists = lists | named
        aimed = named & (facts[:, list_count] == k)[:, None, :]
        codes = jnp.where(aimed, facts[:, list_count + 1][:, None, :], codes)
    earlier = (
        lax.broadcasted_iota(jnp.int32, (row_count, row_count), 0)
        < lax.broadcasted_iota(jnp.int32, (row_count, row_count), 1)
    ).astype(jnp.bfloat16)
    ranks = jnp.einsum(
        "slr,rq->slq", lists.astype(jnp.bfloat16), earlier, preferred_element_type=jnp.float32
    ).astype(jnp.int32)
    rank_iota = lax.broadcasted_iota(jnp.int32, (1, 1, bucket_most, 1), 2)
    holds = lists[:, :, None, :] & (ranks[:, :, None, :] == rank_iota)
    places = holds.astype(jnp.bfloat16)
    slot_codes = jnp.max(jnp.where(holds, codes[:, :, None, :], -1), axis=3)
    normed_all = lax.all_gather(normed, "vocab", axis=0)
    received = jnp.einsum(
        "slmr,srd->slmd", places, normed_all, preferred_element_type=jnp.float32
    ).astype(jnp.bfloat16)
    weight_view = head_weight.reshape(width_dev, blocks_dev, BLK)
    partial_logits = jnp.einsum(
        "slmd,dlt->slmt", received, weight_view, preferred_element_type=jnp.float32
    )
    full_logits = lax.psum(partial_logits, "src")
    slot_top = jnp.max(full_logits, axis=3)
    row_high = jnp.max(jnp.where(holds, slot_top[..., None], MASKED), axis=(1, 2))
    slot_high = jnp.sum(jnp.where(holds, row_high[:, None, None, :], 0.0), axis=3)
    slot_spread = jnp.sum(jnp.exp(full_logits - slot_high[..., None]), axis=3)
    offsets = lax.broadcasted_iota(jnp.int32, full_logits.shape, 3)
    target_hit = offsets == slot_codes[..., None]
    slot_pick = jnp.sum(jnp.where(target_hit, full_logits, 0.0), axis=3)
    row_spread = jnp.sum(jnp.where(holds, slot_spread[..., None], 0.0), axis=(1, 2))
    row_pick = jnp.sum(jnp.where(holds, slot_pick[..., None], 0.0), axis=(1, 2))
    stats = gather_small(jnp.stack([row_high, row_spread, row_pick]), "vocab", 3)
    best = jnp.max(stats[:, 0], axis=0)
    log_total = best + jnp.log(jnp.sum(jnp.exp(stats[:, 0] - best) * stats[:, 1], axis=0))
    row_loss = lax.dynamic_index_in_dim(
        log_total - jnp.sum(stats[:, 2], axis=0), voc_own, axis=0, keepdims=False
    )
    slot_total = jnp.sum(jnp.where(holds, log_total[:, None, None, :], 0.0), axis=3)
    deltas = (
        jnp.exp(full_logits - slot_total[..., None]) - target_hit.astype(jnp.float32)
    ).astype(jnp.bfloat16)
    grad_slots = jnp.einsum(
        "slmt,dlt->slmd", deltas, weight_view, preferred_element_type=jnp.float32
    ).astype(jnp.bfloat16)
    grad_rows = jnp.einsum(
        "slmr,slmd->srd", places, grad_slots, preferred_element_type=jnp.float32
    ).astype(jnp.bfloat16)
    returned = lax.all_to_all(grad_rows, "vocab", split_axis=0, concat_axis=0, tiled=True)
    grad_normed = jnp.sum(returned.astype(jnp.float32), axis=0)
    gained = grad_normed * norm_gain
    sum_g, sum_gx = lax.psum((jnp.sum(gained, axis=1), jnp.sum(gained * centered, axis=1)), "src")
    grad_state = inv_std[:, None] * (
        gained - (sum_g / model_width)[:, None] - centered * (sum_gx / model_width)[:, None]
    )
    return (row_loss, grad_state)


def solution(mesh):
    placed = (
        P("vocab", "src"),
        P("vocab", None, "src"),
        P("vocab", None, "src"),
        P("vocab"),
        P("src", None),
        P("vocab", "src"),
        P("src"),
        P("src"),
        P("src", "vocab"),
        P("vocab", None),
        P("vocab"),
        P("vocab"),
    )
    return jax.shard_map(
        shards,
        mesh=mesh,
        in_specs=placed,
        out_specs=(P("vocab"), P("vocab", "src")),
        check_vma=False,
    )
```

```python
import functools
import math

import jax
import jax.numpy as jnp
from jax import lax
from jax.experimental import pallas as pl
from jax.experimental.pallas import tpu as pltpu
from jax.sharding import PartitionSpec as P

HD = 128
BLK = 128


MASKED = -1e30
EPSILON = 1e-05


VMEM_BYTES = 40 * 1024 * 1024
MESH_ID = pl.DeviceIdType.MESH


def greet(axis, partners):
    barrier = pltpu.get_barrier_semaphore()
    for partner in partners:
        pl.semaphore_signal(barrier, inc=1, device_id={axis: partner}, device_id_type=MESH_ID)
    pl.semaphore_wait(barrier, len(partners))


def remote(axis, src, dst, send_sem, recv_sem, partner):
    return pltpu.make_async_remote_copy(
        src_ref=src,
        dst_ref=dst,
        send_sem=send_sem,
        recv_sem=recv_sem,
        device_id={axis: partner},
        device_id_type=MESH_ID,
    )


def gather_body(axis, count, own_ref, all_ref, send_sems, recv_sems):
    me = lax.axis_index(axis)
    partners = [lax.rem(me + step, count) for step in range(1, count)]
    greet(axis, partners)
    copies = []
    for i, partner in enumerate(partners):
        copy = remote(
            axis, own_ref, all_ref.at[me], send_sems.at[i], recv_sems.at[i], partner
        )
        copy.start()
        copies.append(copy)
    all_ref[me] = own_ref[...]
    for copy in copies:
        copy.wait()


def gather_small(own, axis, collective_id):
    count = lax.axis_size(axis)
    return pl.pallas_call(
        functools.partial(gather_body, axis, count),
        out_shape=jax.ShapeDtypeStruct((count,) + own.shape, own.dtype),
        in_specs=[pl.BlockSpec(memory_space=pltpu.VMEM)],
        out_specs=pl.BlockSpec(memory_space=pltpu.VMEM),
        scratch_shapes=[
            pltpu.SemaphoreType.DMA((count - 1,)),
            pltpu.SemaphoreType.DMA((count - 1,)),
        ],
        compiler_params=pltpu.CompilerParams(
            collective_id=collective_id, has_side_effects=True, vmem_limit_bytes=VMEM_BYTES
        ),
    )(own)


def exchange_body(axis, count, own_ref, all_ref, send_sems, recv_sems):
    me = lax.axis_index(axis)
    partners = [lax.rem(me + step, count) for step in range(1, count)]
    greet(axis, partners)
    copies = []
    for i, partner in enumerate(partners):
        copy = remote(
            axis, own_ref.at[partner], all_ref.at[me], send_sems.at[i], recv_sems.at[i], partner
        )
        copy.start()
        copies.append(copy)
    all_ref[me] = own_ref[me]
    for copy in copies:
        copy.wait()


def exchange(own, axis, collective_id):
    count = lax.axis_size(axis)
    return pl.pallas_call(
        functools.partial(exchange_body, axis, count),
        out_shape=jax.ShapeDtypeStruct(own.shape, own.dtype),
        in_specs=[pl.BlockSpec(memory_space=pltpu.VMEM)],
        out_specs=pl.BlockSpec(memory_space=pltpu.VMEM),
        scratch_shapes=[
            pltpu.SemaphoreType.DMA((count - 1,)),
            pltpu.SemaphoreType.DMA((count - 1,)),
        ],
        compiler_params=pltpu.CompilerParams(
            collective_id=collective_id, has_side_effects=True, vmem_limit_bytes=VMEM_BYTES
        ),
    )(own)


def src_places(axis, rings):
    me = lax.axis_index(axis)
    core = lax.rem(me, 2)
    ring = me // 2
    mate = me + 1 - 2 * core
    others = [lax.rem(ring + step, rings) for step in range(1, rings)]
    greet(axis, [mate] + [other * 2 + core for other in others])
    return core, ring, mate, others


def scatter_body(axis, rings, x_ref, o_ref, first, summed, second, sems):
    core, ring, mate, others = src_places(axis, rings)
    targets = others + [ring]
    pairs = []
    for i, target in enumerate(targets):
        copy = remote(
            axis, x_ref.at[target * 2 + 1 - core], first.at[i], sems.at[0, i], sems.at[1, i], mate
        )
        copy.start()
        pairs.append(copy)
    crossings = []
    for i, target in enumerate(others):
        pairs[i].wait_recv()
        summed[i] = x_ref[target * 2 + core] + first[i]
        copy = remote(
            axis, summed.at[i], second.at[i], sems.at[2, i], sems.at[3, i], target * 2 + core
        )
        copy.start()
        crossings.append(copy)
    pairs[-1].wait_recv()
    o_ref[...] = x_ref[ring * 2 + core] + first[rings - 1]
    for i, copy in enumerate(crossings):
        copy.wait_recv()
        o_ref[...] += second[i]
    for copy in pairs + crossings:
        copy.wait_send()


def scatter_sum(chunks, axis, collective_id):
    count = chunks.shape[0]
    rings = count // 2
    piece = chunks.shape[1:]
    crossing = max(rings - 1, 1)
    return pl.pallas_call(
        functools.partial(scatter_body, axis, rings),
        out_shape=jax.ShapeDtypeStruct(piece, chunks.dtype),
        in_specs=[pl.BlockSpec(memory_space=pltpu.VMEM)],
        out_specs=pl.BlockSpec(memory_space=pltpu.VMEM),
        scratch_shapes=[
            pltpu.VMEM((rings,) + piece, chunks.dtype),
            pltpu.VMEM((crossing,) + piece, chunks.dtype),
            pltpu.VMEM((crossing,) + piece, chunks.dtype),
            pltpu.SemaphoreType.DMA((4, rings)),
        ],
        compiler_params=pltpu.CompilerParams(
            collective_id=collective_id, has_side_effects=True, vmem_limit_bytes=VMEM_BYTES
        ),
    )(chunks)


def shards(
    queries,
    enc_keys,
    enc_values,
    source_lengths,
    out_proj,
    dec_state,
    norm_gain,
    norm_bias,
    head_weight,
    shortlist,
    target_slot,
    target_offset,
):
    voc_count = lax.axis_size("vocab")
    row_count = queries.shape[0]
    mem_count = enc_keys.shape[1]
    model_width = out_proj.shape[1]
    width_dev = dec_state.shape[1]
    heads_dev = enc_keys.shape[2] // HD
    facts = gather_small(
        jnp.concatenate([shortlist.T, target_slot[None], target_offset[None]], axis=0), "vocab", 1
    )
    q_heads = queries.reshape(row_count, heads_dev, HD)
    key_heads = enc_keys[0].reshape(mem_count, heads_dev, HD)
    value_heads = enc_values[0].reshape(mem_count, heads_dev, HD)
    scores = jnp.einsum("rhe,phe->hrp", q_heads, key_heads, preferred_element_type=jnp.float32) * (
        1.0 / math.sqrt(HD)
    )
    positions = lax.iota(jnp.int32, mem_count)
    usable = (positions < source_lengths[0])[None, None, :]
    scores = jnp.where(usable, scores, MASKED)
    row_top = jnp.max(scores, axis=-1)
    raw_weights = jnp.where(usable, jnp.exp(scores - row_top[..., None]), 0.0)
    totals = jnp.sum(raw_weights, axis=-1)
    mixture = jnp.einsum(
        "hrp,phe->rhe",
        raw_weights.astype(jnp.bfloat16),
        value_heads,
        preferred_element_type=jnp.float32,
    )
    own_mix = mixture / totals.T[..., None]
    attn_own = own_mix.astype(jnp.bfloat16).reshape(row_count, heads_dev * HD)
    projected = scatter_sum(
        lax.dot_general(
            out_proj, attn_own, (((0,), (1,)), ((), ())), preferred_element_type=jnp.float32
        ).reshape(-1, width_dev, row_count),
        "src",
        2,
    )
    residual = dec_state.astype(jnp.float32) + projected.T
    sum_rows, square_rows = lax.psum(
        (jnp.sum(residual, axis=1), jnp.sum(residual * residual, axis=1)), "src"
    )
    row_mean = sum_rows / model_width
    variance = square_rows / model_width - row_mean * row_mean
    inv_std = lax.rsqrt(variance + EPSILON)
    centered = (residual - row_mean[:, None]) * inv_std[:, None]
    normed = (centered * norm_gain + norm_bias).astype(jnp.bfloat16)
    list_count = shortlist.shape[1]
    blocks_dev = head_weight.shape[1] // BLK
    vocab_blocks = blocks_dev * voc_count
    bucket_most = max(2, 2 * row_count * list_count // vocab_blocks)
    voc_own = lax.axis_index("vocab")
    local_ids = facts[:, :list_count] - voc_own * blocks_dev
    block_iota = lax.broadcasted_iota(jnp.int32, (1, blocks_dev, 1), 1)
    lists = jnp.zeros((voc_count, blocks_dev, row_count), jnp.bool_)
    codes = jnp.full((voc_count, blocks_dev, row_count), -1, jnp.int32)
    for k in range(list_count):
        named = local_ids[:, k][:, None, :] == block_iota
        lists = lists | named
        aimed = named & (facts[:, list_count] == k)[:, None, :]
        codes = jnp.where(aimed, facts[:, list_count + 1][:, None, :], codes)
    earlier = (
        lax.broadcasted_iota(jnp.int32, (row_count, row_count), 0)
        < lax.broadcasted_iota(jnp.int32, (row_count, row_count), 1)
    ).astype(jnp.bfloat16)
    ranks = jnp.einsum(
        "slr,rq->slq", lists.astype(jnp.bfloat16), earlier, preferred_element_type=jnp.float32
    ).astype(jnp.int32)
    rank_iota = lax.broadcasted_iota(jnp.int32, (1, 1, bucket_most, 1), 2)
    holds = lists[:, :, None, :] & (ranks[:, :, None, :] == rank_iota)
    places = holds.astype(jnp.bfloat16)
    slot_codes = jnp.max(jnp.where(holds, codes[:, :, None, :], -1), axis=3)
    normed_all = lax.all_gather(normed, "vocab", axis=0)
    received = jnp.einsum(
        "slmr,srd->slmd", places, normed_all, preferred_element_type=jnp.float32
    ).astype(jnp.bfloat16)
    weight_view = head_weight.reshape(width_dev, blocks_dev, BLK)
    partial_logits = jnp.einsum(
        "slmd,dlt->slmt", received, weight_view, preferred_element_type=jnp.float32
    )
    full_logits = lax.psum(partial_logits, "src")
    slot_top = jnp.max(full_logits, axis=3)
    row_high = jnp.max(jnp.where(holds, slot_top[..., None], MASKED), axis=(1, 2))
    slot_high = jnp.sum(jnp.where(holds, row_high[:, None, None, :], 0.0), axis=3)
    slot_spread = jnp.sum(jnp.exp(full_logits - slot_high[..., None]), axis=3)
    offsets = lax.broadcasted_iota(jnp.int32, full_logits.shape, 3)
    target_hit = offsets == slot_codes[..., None]
    slot_pick = jnp.sum(jnp.where(target_hit, full_logits, 0.0), axis=3)
    row_spread = jnp.sum(jnp.where(holds, slot_spread[..., None], 0.0), axis=(1, 2))
    row_pick = jnp.sum(jnp.where(holds, slot_pick[..., None], 0.0), axis=(1, 2))
    stats = gather_small(jnp.stack([row_high, row_spread, row_pick]), "vocab", 3)
    best = jnp.max(stats[:, 0], axis=0)
    log_total = best + jnp.log(jnp.sum(jnp.exp(stats[:, 0] - best) * stats[:, 1], axis=0))
    row_loss = lax.dynamic_index_in_dim(
        log_total - jnp.sum(stats[:, 2], axis=0), voc_own, axis=0, keepdims=False
    )
    slot_total = jnp.sum(jnp.where(holds, log_total[:, None, None, :], 0.0), axis=3)
    deltas = (
        jnp.exp(full_logits - slot_total[..., None]) - target_hit.astype(jnp.float32)
    ).astype(jnp.bfloat16)
    grad_slots = jnp.einsum(
        "slmt,dlt->slmd", deltas, weight_view, preferred_element_type=jnp.float32
    ).astype(jnp.bfloat16)
    grad_rows = jnp.einsum(
        "slmr,slmd->srd", places, grad_slots, preferred_element_type=jnp.float32
    ).astype(jnp.bfloat16)
    returned = exchange(grad_rows, "vocab", 4)
    grad_normed = jnp.sum(returned.astype(jnp.float32), axis=0)
    gained = grad_normed * norm_gain
    sum_g, sum_gx = lax.psum((jnp.sum(gained, axis=1), jnp.sum(gained * centered, axis=1)), "src")
    grad_state = inv_std[:, None] * (
        gained - (sum_g / model_width)[:, None] - centered * (sum_gx / model_width)[:, None]
    )
    return (row_loss, grad_state)


def solution(mesh):
    placed = (
        P("vocab", "src"),
        P("vocab", None, "src"),
        P("vocab", None, "src"),
        P("vocab"),
        P("src", None),
        P("vocab", "src"),
        P("src"),
        P("src"),
        P("src", "vocab"),
        P("vocab", None),
        P("vocab"),
        P("vocab"),
    )
    return jax.shard_map(
        shards,
        mesh=mesh,
        in_specs=placed,
        out_specs=(P("vocab"), P("vocab", "src")),
        check_vma=False,
    )
```
